32 devices in a mesh: seq: 8 (over z, y), head: 4 (over x, core).
Axes of the slice: x: 2, y: 2, z: 4, core: 2. Of those that a mesh axis runs over, the one named last changes fastest.
Arguments:
- queries: bfloat16 [16384, 4096], P('seq', 'head'), may hold values from -6 to 6
- key_inputs: bfloat16 [16384, 4096], P('seq', 'head'), may hold values from -6 to 6
- values: bfloat16 [16384, 4096], P('seq', 'head'), may hold values from -36 to 36
- out_gain: float32 [4096], replicated, may hold values from 0.25 to 1.75
Outputs:
- normed: bfloat16 [16384, 4096], P(('seq', 'head'))
The draws below stay inside these ranges and needn't reach their ends.
All inputs are finite; a program needn't handle non-finite values.
Results may differ from the reference program's by a relative error of at most 0.0056.
Values may be sent and summed in bfloat16 or wider, within the bound.
A program may use at most 64 MiB of HBM per device.

```python
import math
import jax
import jax.numpy as jnp
from jax import lax

HEADS = 32
HD = 128
BLOCK = 512
TOKENS = 16384


def draw_values(key, part):
    key_rows, key_cols, key_noise = jax.random.split(key, 3)
    features = HEADS * HD
    row_scale = jnp.exp(jax.random.uniform(key_rows, (TOKENS, 1), jnp.float32, math.log(0.3), math.log(3.0)))
    col_scale = jnp.exp(jax.random.uniform(key_cols, (1, features), jnp.float32, math.log(0.3), math.log(3.0)))
    base = jnp.clip(jax.random.normal(key_noise, (TOKENS, features), jnp.float32), -4.0, 4.0)
    return (row_scale * col_scale * base).astype(jnp.bfloat16)


def level_of(key, shape, shards, smallest, top_value):
    loudness = 1.0
    for dim, shards_of in shards:
        steps = jax.random.uniform(jax.random.fold_in(jax.random.fold_in(key, 6), dim), (shards_of,), jnp.float32, smallest / len(shards), top_value / len(shards))
        loudness = loudness * jnp.repeat(jnp.exp(steps), shape[dim] // shards_of).reshape((-1,) + (1,) * (len(shape) - 1 - dim))
    return loudness


def bell_draw(own_key, extent, width, limit, pieces=(), held_as=jnp.bfloat16):
    array = jax.random.normal(own_key, extent, jnp.float32) * width
    if len(pieces) > 0:
        array = level_of(own_key, extent, pieces, -0.22, 0.18) * array
    return jnp.clip(array, min=-limit, max=limit).astype(held_as)


def setup_inputs(seed: int = 0) -> dict:
    key_list = jax.random.split(jax.random.key(seed), 5)
    queries = bell_draw(key_list[0], (TOKENS, HEADS * HD), 1.0, 6.0, ((0, 8), (1, 4)))
    key_inputs = bell_draw(key_list[1], (TOKENS, HEADS * HD), 1.0, 6.0, ((0, 8), (1, 4)))
    values = draw_values(jax.random.fold_in(key_list[4], 71), 0)
    out_gain = jnp.clip(1.0 + 0.15 * jax.random.normal(key_list[3], (HEADS * HD,), jnp.float32), 0.25, 1.75)
    return dict(queries=queries, key_inputs=key_inputs, values=values, out_gain=out_gain)


def reference(queries, key_inputs, values, out_gain):
    token_count = queries.shape[0]
    block_count = token_count // BLOCK
    query_map = jax.nn.silu(queries.astype(jnp.float32)).astype(jnp.bfloat16)
    key_map = jax.nn.silu(key_inputs.astype(jnp.float32)).astype(jnp.bfloat16)
    causal = jnp.tril(jnp.ones((BLOCK, BLOCK), dtype=bool))

    def head_fn(head_index):
        first = (head_index * HD).astype(jnp.int32)
        head_queries = lax.dynamic_slice_in_dim(query_map, first, HD, 1).reshape(block_count, BLOCK, HD)
        head_keys = lax.dynamic_slice_in_dim(key_map, first, HD, 1).reshape(block_count, BLOCK, HD)
        head_values = lax.dynamic_slice_in_dim(values, first, HD, 1).reshape(block_count, BLOCK, HD)

        def advance(carry_state, blocks):
            block_queries, block_keys, block_values = blocks
            scores = jnp.dot(block_queries, block_keys.T, preferred_element_type=jnp.float32)
            scores = jnp.where(causal, scores, 0.0).astype(jnp.bfloat16)
            inside = jnp.dot(scores, block_values, preferred_element_type=jnp.float32)
            carried = jnp.dot(block_queries.astype(jnp.float32), carry_state, precision=lax.Precision.HIGHEST)
            carry_state = carry_state + jnp.dot(block_keys.T, block_values, preferred_element_type=jnp.float32)
            return (carry_state, (inside + carried).astype(jnp.bfloat16))
        _, head_outputs = lax.scan(advance, jnp.zeros((HD, HD), jnp.float32), (head_queries, head_keys, head_values))
        return head_outputs.reshape(token_count, HD)
    all_heads = lax.map(head_fn, jnp.arange(HEADS, dtype=jnp.int32))
    attended = jnp.transpose(all_heads, (1, 0, 2)).reshape(token_count, HEADS * HD)
    wide_out = attended.astype(jnp.float32)
    mean_square = lax.optimization_barrier(jnp.mean(wide_out * wide_out, axis=1, keepdims=True))
    return (wide_out * lax.rsqrt(mean_square + 1e-06) * out_gain.astype(jnp.float32)).astype(jnp.bfloat16)
```

```python
import functools

import jax
import jax.numpy as jnp
from jax import lax
from jax.experimental import pallas as pl
from jax.experimental.pallas import tpu as pltpu
from jax.sharding import PartitionSpec as P

HD = 128
BLOCK = 512
SUB = 256
EPS = 1e-06
FIRST = 2
STEP = 2
NORM_ROWS = 128
MESH = pl.DeviceIdType.MESH


def silu(u):
    wide = u.astype(jnp.float32)
    return (wide * (0.5 + 0.5 * jnp.tanh(0.5 * wide))).astype(jnp.bfloat16)


def attend_kernel(
    seq_n, head_n, q_hbm, k_hbm, v_hbm, out,
    qb, kb, vb, att, before, own, near, far, onward, prefix,
    load_sem, near_send, near_recv, far_send, far_recv, out_send, out_recv, keep_sem,
):
    heads, rows = qb.shape[0], qb.shape[1]
    blocks = rows // BLOCK
    chunk = rows // head_n
    pairs = seq_n // 2
    chips = head_n // 2
    s, me = lax.axis_index("seq"), lax.axis_index("head")
    pair, odd = s // 2, s % 2
    partner = s + 1 - 2 * odd

    def peer(k):
        return ((me // 2 + chips - 1 - k // 2) % chips) * 2 + (me % 2 + 1 - k % 2) % 2

    barrier = pltpu.get_barrier_semaphore()

    def greet(device):
        pl.semaphore_signal(barrier, inc=1, device_id=device, device_id_type=MESH)

    greet({"seq": partner})
    for k in range(head_n - 1):
        greet({"head": peer(k)})

    @pl.when(pair > 0)
    def _():
        greet({"seq": s - 2})

    @pl.when(pair < pairs - 1)
    def _():
        greet({"seq": s + 2})

    def load(which, h):
        src = (q_hbm, k_hbm, v_hbm)[which]
        dst = (qb, kb, vb)[which]
        cols = pl.ds(pl.multiple_of(h * HD, HD), HD)
        return pltpu.make_async_copy(src.at[:, cols], dst.at[h], load_sem.at[which, h])

    for which in (1, 2, 0):
        for h in range(heads):
            if which == 2:
                continue
            load(which, h).start()
            if which == 1:
                load(2, h).start()

    pl.semaphore_wait(
        barrier, head_n + (pair > 0).astype(jnp.int32) + (pair < pairs - 1).astype(jnp.int32)
    )

    def near_copy(h):
        return pltpu.make_async_remote_copy(
            src_ref=own.at[h], dst_ref=near.at[h], send_sem=near_send.at[h],
            recv_sem=near_recv.at[h], device_id={"seq": partner}, device_id_type=MESH,
        )

    def far_copy(h):
        return pltpu.make_async_remote_copy(
            src_ref=onward.at[h], dst_ref=far.at[h], send_sem=far_send.at[h],
            recv_sem=far_recv.at[h], device_id={"seq": s + 2}, device_id_type=MESH,
        )

    def out_copy(h, d):
        first = pl.multiple_of(d * chunk, chunk)
        return pltpu.make_async_remote_copy(
            src_ref=att.at[h, pl.ds(first, chunk)], dst_ref=out.at[me * heads + h],
            send_sem=out_send.at[d, h], recv_sem=out_recv.at[me, h],
            device_id={"head": d}, device_id_type=MESH,
        )

    def in_copy(h, d):
        return pltpu.make_async_remote_copy(
            src_ref=att.at[h, pl.ds(0, chunk)], dst_ref=out.at[d * heads + h],
            send_sem=out_send.at[d, h], recv_sem=out_recv.at[d, h],
            device_id={"head": d}, device_id_type=MESH,
        )

    def keep_copy(h):
        first = pl.multiple_of(me * chunk, chunk)
        return pltpu.make_async_copy(
            att.at[h, pl.ds(first, chunk)], out.at[me * heads + h], keep_sem.at[h]
        )

    def state(h):
        load(1, h).wait()
        load(2, h).wait()
        run = jnp.zeros((HD, HD), jnp.float32)
        for b in range(blocks):
            here = pl.ds(b * BLOCK, BLOCK)
            keys = silu(kb[h, here])
            kb[h, here] = keys
            before[h, b] = run
            run = run + lax.dot_general(
                keys, vb[h, here], (((0,), (0,)), ((), ())), preferred_element_type=jnp.float32
            )
        own[h] = run
        near_copy(h).start()

    def chain(h):
        near_copy(h).wait_recv()
        other = near[h]

        @pl.when(pair > 0)
        def _():
            far_copy(h).wait_recv()

        @pl.when(pair == 0)
        def _():
            far[h] = jnp.zeros((HD, HD), jnp.float32)

        earlier = far[h]

        @pl.when(pair < pairs - 1)
        def _():
            onward[h] = earlier + (own[h] + other)
            far_copy(h).start()

        prefix[h] = earlier + odd.astype(jnp.float32) * other

    def attend(h, row, offset, keys_seen, count, split):
        queries = silu(qb[h, pl.ds(row, count)])
        start = row - offset
        seen = pl.ds(start, keys_seen)
        scores = lax.dot_general(
            queries, kb[h, seen], (((1,), (1,)), ((), ())), preferred_element_type=jnp.float32
        )
        t_pos = lax.broadcasted_iota(jnp.int32, scores.shape, 0) + offset
        s_pos = lax.broadcasted_iota(jnp.int32, scores.shape, 1)
        weights = jnp.where(s_pos <= t_pos, scores, 0.0).astype(jnp.bfloat16)
        total = jnp.dot(weights, vb[h, seen], preferred_element_type=jnp.float32)
        twice = jnp.concatenate([queries, queries], axis=1)
        total = total + jnp.dot(twice, split, preferred_element_type=jnp.float32)
        att[h, pl.ds(row, count)] = total.astype(jnp.bfloat16)

    def split_state(h, b):
        whole = prefix[h] + before[h, b]
        high = whole.astype(jnp.bfloat16)
        low = (whole - high.astype(jnp.float32)).astype(jnp.bfloat16)
        return jnp.concatenate([high, low], axis=0)

    def finish(h):
        load(0, h).wait()

        def serve(k, carry):
            d = peer(k)
            if chunk % BLOCK == 0:
                per = chunk // BLOCK
                for j in range(per):
                    b = d * per + j
                    first = pl.multiple_of(b * BLOCK, BLOCK)
                    split = split_state(h, b)
                    for t in range(BLOCK // SUB):
                        attend(h, first + t * SUB, t * SUB, (t + 1) * SUB, SUB, split)
            else:
                per = BLOCK // chunk
                first = pl.multiple_of(d * chunk, chunk)
                attend(h, first, (d % per) * chunk, BLOCK, chunk, split_state(h, d // per))

            @pl.when(k < head_n - 1)
            def _():
                out_copy(h, d).start()

            @pl.when(k == head_n - 1)
            def _():
                keep_copy(h).start()

            return carry

        lax.fori_loop(0, head_n, serve, 0)

    finish_from = FIRST + STEP * (pairs - 1)

    def slot(i, carry):
        @pl.when(i < heads)
        def _():
            state(i)

        linked = i - FIRST - STEP * pair

        @pl.when((linked >= 0) & (linked < heads))
        def _():
            chain(linked)

        @pl.when((i >= finish_from) & (i < finish_from + heads))
        def _():
            finish(i - finish_from)

        return carry

    lax.fori_loop(0, max(heads, finish_from + heads), slot, 0)

    def drain(h, carry):
        near_copy(h).wait_send()

        @pl.when(pair < pairs - 1)
        def _():
            far_copy(h).wait_send()

        keep_copy(h).wait()
        for k in range(head_n - 1):
            out_copy(h, peer(k)).wait_send()
            in_copy(h, peer(k)).wait_recv()
        return carry

    lax.fori_loop(0, heads, drain, 0)


def norm_kernel(att_ref, gain_ref, out_ref):
    total_heads, rows = att_ref.shape[0], att_ref.shape[1]
    squares = jnp.zeros((rows, HD), jnp.float32)
    for h in range(total_heads):
        wide = att_ref[h].astype(jnp.float32)
        squares = squares + wide * wide
    mean_square = jnp.sum(squares, axis=1, keepdims=True) * (1.0 / (total_heads * HD))
    scale = lax.rsqrt(mean_square + EPS)
    for h in range(total_heads):
        cols = pl.ds(h * HD, HD)
        wide = att_ref[h].astype(jnp.float32)
        out_ref[:, cols] = (wide * scale * gain_ref[:, cols]).astype(jnp.bfloat16)


def shards(seq_n, head_n, queries, key_inputs, values, out_gain):
    rows, features = queries.shape
    heads = features // HD
    chunk = rows // head_n
    total_heads = heads * head_n
    half = pltpu.VMEM((heads, rows, HD), jnp.bfloat16)
    square = pltpu.VMEM((heads, HD, HD), jnp.float32)
    dma = pltpu.SemaphoreType.DMA
    attended = pl.pallas_call(
        functools.partial(attend_kernel, seq_n, head_n),
        out_shape=jax.ShapeDtypeStruct((total_heads, chunk, HD), jnp.bfloat16),
        in_specs=[pl.BlockSpec(memory_space=pl.ANY)] * 3,
        out_specs=pl.BlockSpec(memory_space=pl.ANY),
        scratch_shapes=[
            half, half, half, half,
            pltpu.VMEM((heads, rows // BLOCK, HD, HD), jnp.float32),
            square, square, square, square, square,
            dma((3, heads)), dma((heads,)), dma((heads,)), dma((heads,)), dma((heads,)),
            dma((head_n, heads)), dma((head_n, heads)), dma((heads,)),
        ],
        compiler_params=pltpu.CompilerParams(
            collective_id=0, has_side_effects=True, vmem_limit_bytes=52 * 1024 * 1024
        ),
        name="attend",
    )(queries, key_inputs, values)
    step_rows = min(NORM_ROWS, chunk)
    return pl.pallas_call(
        norm_kernel,
        grid=(chunk // step_rows,),
        out_shape=jax.ShapeDtypeStruct((chunk, total_heads * HD), jnp.bfloat16),
        in_specs=[
            pl.BlockSpec((total_heads, step_rows, HD), lambda i: (0, i, 0)),
            pl.BlockSpec((1, total_heads * HD), lambda i: (0, 0)),
        ],
        out_specs=pl.BlockSpec((step_rows, total_heads * HD), lambda i: (i, 0)),
        compiler_params=pltpu.CompilerParams(vmem_limit_bytes=32 * 1024 * 1024),
        name="norm",
    )(attended, out_gain.reshape(1, -1))


def solution(mesh):
    return jax.shard_map(
        functools.partial(shards, mesh.shape["seq"], mesh.shape["head"]),
        mesh=mesh,
        in_specs=(P("seq", "head"), P("seq", "head"), P("seq", "head"), P()),
        out_specs=P(("seq", "head"), None),
        check_vma=False,
    )
```

```python
import functools

import jax
import jax.numpy as jnp
from jax import lax
from jax.experimental import pallas as pl
from jax.experimental.pallas import tpu as pltpu
from jax.sharding import PartitionSpec as P

HD = 128
BLOCK = 512
SUB = 256
EPS = 1e-06
FIRST = 1
STEP = 1
BANDS = 4
NORM_ROWS = 64
MESH = pl.DeviceIdType.MESH


def silu(u):
    wide = u.astype(jnp.float32)
    return (wide * (0.5 + 0.5 * jnp.tanh(0.5 * wide))).astype(jnp.bfloat16)


def attend_kernel(
    seq_n, head_n, q_hbm, k_hbm, v_hbm, out,
    qb, kb, vb, att, before, own, near, far, onward, prefix,
    load_sem, near_send, near_recv, far_send, far_recv, out_send, out_recv, keep_sem,
):
    heads, rows = qb.shape[0], qb.shape[1]
    blocks = rows // BLOCK
    chunk = rows // head_n
    pairs = seq_n // 2
    chips = head_n // 2
    s, me = lax.axis_index("seq"), lax.axis_index("head")
    pair, odd = s // 2, s % 2
    partner = s + 1 - 2 * odd

    def peer(k):
        return ((me // 2 + chips - 1 - k // 2) % chips) * 2 + (me % 2 + 1 - k % 2) % 2

    barrier = pltpu.get_barrier_semaphore()

    def greet(device):
        pl.semaphore_signal(barrier, inc=1, device_id=device, device_id_type=MESH)

    greet({"seq": partner})
    for k in range(head_n - 1):
        greet({"head": peer(k)})

    @pl.when(pair > 0)
    def _():
        greet({"seq": s - 2})

    @pl.when(pair < pairs - 1)
    def _():
        greet({"seq": s + 2})

    def load(which, h):
        src = (q_hbm, k_hbm, v_hbm)[which]
        dst = (qb, kb, vb)[which]
        cols = pl.ds(pl.multiple_of(h * HD, HD), HD)
        return pltpu.make_async_copy(src.at[:, cols], dst.at[h], load_sem.at[which, h])

    for which in (1, 2, 0):
        for h in range(heads):
            if which == 2:
                continue
            load(which, h).start()
            if which == 1:
                load(2, h).start()

    pl.semaphore_wait(
        barrier, head_n + (pair > 0).astype(jnp.int32) + (pair < pairs - 1).astype(jnp.int32)
    )

    def band(c):
        return pl.ds(c * (HD // BANDS), HD // BANDS)

    def near_copy(h, c):
        return pltpu.make_async_remote_copy(
            src_ref=own.at[h, band(c)], dst_ref=near.at[h, band(c)], send_sem=near_send.at[c, h],
            recv_sem=near_recv.at[c, h], device_id={"seq": partner}, device_id_type=MESH,
        )

    def far_copy(h, c):
        return pltpu.make_async_remote_copy(
            src_ref=onward.at[h, band(c)], dst_ref=far.at[h, band(c)], send_sem=far_send.at[c, h],
            recv_sem=far_recv.at[c, h], device_id={"seq": s + 2}, device_id_type=MESH,
        )

    def out_copy(h, d):
        first = pl.multiple_of(d * chunk, chunk)
        return pltpu.make_async_remote_copy(
            src_ref=att.at[h, pl.ds(first, chunk)], dst_ref=out.at[me * heads + h],
            send_sem=out_send.at[d, h], recv_sem=out_recv.at[me, h],
            device_id={"head": d}, device_id_type=MESH,
        )

    def in_copy(h, d):
        return pltpu.make_async_remote_copy(
            src_ref=att.at[h, pl.ds(0, chunk)], dst_ref=out.at[d * heads + h],
            send_sem=out_send.at[d, h], recv_sem=out_recv.at[d, h],
            device_id={"head": d}, device_id_type=MESH,
        )

    def keep_copy(h):
        first = pl.multiple_of(me * chunk, chunk)
        return pltpu.make_async_copy(
            att.at[h, pl.ds(first, chunk)], out.at[me * heads + h], keep_sem.at[h]
        )

    def state(h):
        load(1, h).wait()
        load(2, h).wait()
        run = jnp.zeros((HD, HD), jnp.float32)
        for b in range(blocks):
            here = pl.ds(b * BLOCK, BLOCK)
            keys = silu(kb[h, here])
            kb[h, here] = keys
            before[h, b] = run
            run = run + lax.dot_general(
                keys, vb[h, here], (((0,), (0,)), ((), ())), preferred_element_type=jnp.float32
            )
        own[h] = run
        for c in range(BANDS):
            near_copy(h, c).start()

    def chain(h):
        for c in range(BANDS):
            near_copy(h, c).wait_recv()
            other = near[h, band(c)]

            @pl.when(pair > 0)
            def _():
                far_copy(h, c).wait_recv()

            @pl.when(pair == 0)
            def _():
                far[h, band(c)] = jnp.zeros_like(other)

            earlier = far[h, band(c)]

            @pl.when(pair < pairs - 1)
            def _():
                onward[h, band(c)] = earlier + (own[h, band(c)] + other)
                far_copy(h, c).start()

            prefix[h, band(c)] = earlier + odd.astype(jnp.float32) * other

    def attend(h, row, offset, keys_seen, count, split):
        queries = silu(qb[h, pl.ds(row, count)])
        start = row - offset
        seen = pl.ds(start, keys_seen)
        scores = lax.dot_general(
            queries, kb[h, seen], (((1,), (1,)), ((), ())), preferred_element_type=jnp.float32
        )
        t_pos = lax.broadcasted_iota(jnp.int32, scores.shape, 0) + offset
        s_pos = lax.broadcasted_iota(jnp.int32, scores.shape, 1)
        weights = jnp.where(s_pos <= t_pos, scores, 0.0).astype(jnp.bfloat16)
        total = jnp.dot(weights, vb[h, seen], preferred_element_type=jnp.float32)
        twice = jnp.concatenate([queries, queries], axis=1)
        total = total + jnp.dot(twice, split, preferred_element_type=jnp.float32)
        att[h, pl.ds(row, count)] = total.astype(jnp.bfloat16)

    def split_state(h, b):
        whole = prefix[h] + before[h, b]
        high = whole.astype(jnp.bfloat16)
        low = (whole - high.astype(jnp.float32)).astype(jnp.bfloat16)
        return jnp.concatenate([high, low], axis=0)

    def finish(h):
        load(0, h).wait()

        def serve(k, carry):
            d = peer(k)
            if chunk % BLOCK == 0:
                per = chunk // BLOCK
                for j in range(per):
                    b = d * per + j
                    first = pl.multiple_of(b * BLOCK, BLOCK)
                    split = split_state(h, b)
                    for t in range(BLOCK // SUB):
                        attend(h, first + t * SUB, t * SUB, (t + 1) * SUB, SUB, split)
            else:
                per = BLOCK // chunk
                first = pl.multiple_of(d * chunk, chunk)
                attend(h, first, (d % per) * chunk, BLOCK, chunk, split_state(h, d // per))

            @pl.when(k < head_n - 1)
            def _():
                out_copy(h, d).start()

            @pl.when(k == head_n - 1)
            def _():
                keep_copy(h).start()

            return carry

        lax.fori_loop(0, head_n, serve, 0)

    finish_from = FIRST + STEP * (pairs - 1)

    def slot(i, carry):
        @pl.when(i < heads)
        def _():
            state(i)

        linked = i - FIRST - STEP * pair

        @pl.when((linked >= 0) & (linked < heads))
        def _():
            chain(linked)

        @pl.when((i >= finish_from) & (i < finish_from + heads))
        def _():
            finish(i - finish_from)

        return carry

    lax.fori_loop(0, max(heads, finish_from + heads), slot, 0)

    def drain(h, carry):
        for c in range(BANDS):
            near_copy(h, c).wait_send()

        @pl.when(pair < pairs - 1)
        def _():
            for c in range(BANDS):
                far_copy(h, c).wait_send()

        keep_copy(h).wait()
        for k in range(head_n - 1):
            out_copy(h, peer(k)).wait_send()
            in_copy(h, peer(k)).wait_recv()
        return carry

    lax.fori_loop(0, heads, drain, 0)


def norm_kernel(att_ref, gain_ref, out_hbm, staged, sems):
    total_heads, rows = att_ref.shape[0], att_ref.shape[1]
    step = rows // sems.shape[0]

    def store(i):
        here = pl.ds(i * step, step)
        return pltpu.make_async_copy(staged.at[here], out_hbm.at[here], sems.at[i])

    for i in range(rows // step):
        here = pl.ds(i * step, step)
        squares = jnp.zeros((step, HD), jnp.float32)
        for h in range(total_heads):
            wide = att_ref[h, here].astype(jnp.float32)
            squares = squares + wide * wide
        mean_square = jnp.sum(squares, axis=1, keepdims=True) * (1.0 / (total_heads * HD))
        scale = jnp.broadcast_to(lax.rsqrt(mean_square + EPS), squares.shape)
        for h in range(total_heads):
            cols = pl.ds(h * HD, HD)
            wide = att_ref[h, here].astype(jnp.float32)
            staged[here, cols] = (wide * scale * gain_ref[:, cols]).astype(jnp.bfloat16)
        store(i).start()
    for i in range(rows // step):
        store(i).wait()


def shards(seq_n, head_n, queries, key_inputs, values, out_gain):
    rows, features = queries.shape
    heads = features // HD
    chunk = rows // head_n
    total_heads = heads * head_n
    half = pltpu.VMEM((heads, rows, HD), jnp.bfloat16)
    square = pltpu.VMEM((heads, HD, HD), jnp.float32)
    dma = pltpu.SemaphoreType.DMA
    attended = pl.pallas_call(
        functools.partial(attend_kernel, seq_n, head_n),
        out_shape=jax.ShapeDtypeStruct((total_heads, chunk, HD), jnp.bfloat16),
        in_specs=[pl.BlockSpec(memory_space=pltpu.HBM)] * 3,
        out_specs=pl.BlockSpec(memory_space=pltpu.VMEM),
        scratch_shapes=[
            half, half, half, half,
            pltpu.VMEM((heads, rows // BLOCK, HD, HD), jnp.float32),
            square, square, square, square, square,
            dma((3, heads)), dma((BANDS, heads)), dma((BANDS, heads)),
            dma((BANDS, heads)), dma((BANDS, heads)),
            dma((head_n, heads)), dma((head_n, heads)), dma((heads,)),
        ],
        compiler_params=pltpu.CompilerParams(
            collective_id=0, has_side_effects=True, vmem_limit_bytes=48 * 1024 * 1024
        ),
        name="attend",
    )(queries, key_inputs, values)
    step_rows = min(NORM_ROWS, chunk)
    return pl.pallas_call(
        norm_kernel,
        out_shape=jax.ShapeDtypeStruct((chunk, total_heads * HD), jnp.bfloat16),
        in_specs=[pl.BlockSpec(memory_space=pltpu.VMEM)] * 2,
        out_specs=pl.BlockSpec(memory_space=pltpu.HBM),
        scratch_shapes=[
            pltpu.VMEM((chunk, total_heads * HD), jnp.bfloat16), dma((chunk // step_rows,)),
        ],
        compiler_params=pltpu.CompilerParams(vmem_limit_bytes=32 * 1024 * 1024),
        name="norm",
    )(attended, out_gain.reshape(1, -1))


def solution(mesh):
    return jax.shard_map(
        functools.partial(shards, mesh.shape["seq"], mesh.shape["head"]),
        mesh=mesh,
        in_specs=(P("seq", "head"), P("seq", "head"), P("seq", "head"), P()),
        out_specs=P(("seq", "head"), None),
        check_vma=False,
    )
```
